256 devices in a mesh: lat: 32 (over z, y_lo, core), lon: 8 (over x, y_hi).
Axes of the slice: x: 4, y: 4 (y_hi: 2, y_lo: 2; y = y_hi * 2 + y_lo), z: 8, core: 2. Of those that a mesh axis runs over, the one named last changes fastest.
Arguments:
- increment: float32 [2, 6, 768, 4096], P(None, None, 'lat', 'lon'), may hold values from -6 to 6
- normal_gain: float32 [2, 6, 768, 4096], P(None, None, 'lat', 'lon'), may hold values from 0.5 to 2
- coef_x: float32 [6, 768, 4096], P(None, 'lat', 'lon'), may hold values from 0.08 to 0.12
- coef_y: float32 [6, 768, 4096], P(None, 'lat', 'lon'), may hold values from 0.08 to 0.12
- ocean: int32 [6, 768, 4096], P(None, 'lat', 'lon'), may hold values 0 or 1
- inv_area: float32 [768, 4096], P('lat', 'lon'), may hold values from 1.6 to 2
- partner: int32 [4096], replicated, may hold values from 0 to 4095, as said below
Outputs:
- adjoint_field: float32 [2, 6, 768, 4096], P(None, None, 'lat', 'lon')
The draws below stay inside these ranges and needn't reach their ends.
Inputs may be any that keep to these rules, and one draw needn't show every extreme that they name: partner[i] = (c - i) mod 4096 for one c drawn per draw, so partner[partner[i]] = i.
All inputs are finite; a program needn't handle non-finite values. No bound on the sum of `ocean` on one device may be relied on, other than what follows from the above.
Results may differ from the reference program's by a relative error of at most 0.00002.
Values sent between devices are 32-bit elements; how exact they have to be, the bound alone decides.
A program may use at most 64 MiB of HBM per device.

```python
import math
import jax
import jax.numpy as jnp
from jax import lax

LEV = 6
ITERS = 10
NY = 768
NX = 4096


def draw_partner(key, part):
    key = jax.random.fold_in(key, 7)
    pivot = jax.random.randint(key, (), 0, NX, dtype=jnp.int32)
    return jnp.mod(pivot - jnp.arange(NX, dtype=jnp.int32), NX).astype(jnp.int32)


def draw_increment(key, part):
    key = jax.random.fold_in(key, 11)
    size_key, sign_key = jax.random.split(key)
    shape = (2, LEV, NY, NX)
    flips = jax.random.uniform(sign_key, shape, jnp.float32)
    signs = jnp.where(flips < 0.5, -1.0, 1.0)
    sizes = jax.random.uniform(size_key, shape, jnp.float32, 2.0, 6.0)
    return (signs * sizes).astype(jnp.float32)


def draw_coef_x(key, part):
    key = jax.random.fold_in(key, 13)
    return jax.random.uniform(key, (LEV, NY, NX), jnp.float32, 0.08, 0.12)


def draw_coef_y(key, part):
    key = jax.random.fold_in(key, 17)
    return jax.random.uniform(key, (LEV, NY, NX), jnp.float32, 0.08, 0.12)


def draw_inv_area(key, part):
    key = jax.random.fold_in(key, 19)
    return jax.random.uniform(key, (NY, NX), jnp.float32, 1.6, 2.0)


def set_ends(array, own_key, low, top_value):
    longest = array.shape.index(max(array.shape))
    spots = []
    for shift in (0, 1):
        where = [jax.random.randint(jax.random.fold_in(own_key, axis), (), 0, length) for axis, length in enumerate(array.shape)]
        where[longest] = (where[longest] + shift) % array.shape[longest]
        spots.append(tuple(where))
    return array.at[spots[0]].set(low).at[spots[1]].set(top_value)


def steps_of(key, dims, pieces, least, high):
    factor_of = 1.0
    for dim, blocks in pieces:
        draws = jax.random.uniform(jax.random.fold_in(jax.random.fold_in(key, 6), dim), (blocks,), jnp.float32, least / len(pieces), high / len(pieces))
        factor_of = factor_of * jnp.repeat(jnp.exp(draws), dims[dim] // blocks).reshape((-1,) + (1,) * (len(dims) - 1 - dim))
    return factor_of


def setup_inputs(seed: int = 0) -> dict:
    arg_keys = jax.random.split(jax.random.key(seed), 8)
    increment = draw_increment(jax.random.fold_in(arg_keys[7], 71), 0)
    normal_gain = jnp.clip(jnp.exp(math.log(2.0) - 1.3862944 * jax.random.uniform(arg_keys[1], (2, LEV, NY, NX), jnp.float32) ** steps_of(arg_keys[1], (2, LEV, NY, NX), ((2, 32), (3, 8)), -0.2, 0.2)), 0.5, 2.0)
    coef_x = draw_coef_x(jax.random.fold_in(arg_keys[7], 71), 0)
    coef_y = draw_coef_y(jax.random.fold_in(arg_keys[7], 71), 0)
    ocean = set_ends((jax.random.randint(arg_keys[4], (LEV, NY, NX), 0, 10) < 9).astype(jnp.int32), jax.random.fold_in(arg_keys[4], 1), 0, 1)
    inv_area = draw_inv_area(jax.random.fold_in(arg_keys[7], 71), 0)
    partner = draw_partner(jax.random.fold_in(arg_keys[7], 71), 0)
    return {"increment": increment, "normal_gain": normal_gain, "coef_x": coef_x, "coef_y": coef_y, "ocean": ocean, "inv_area": inv_area, "partner": partner}


def level_adjoint(inputs, inv_area, partner):
    values, gains, coef_x, coef_y, ocean = inputs
    mf = ocean.astype(jnp.float32)
    ex = coef_x * mf * jnp.roll(mf, -1, axis=1)
    zero_row = jnp.zeros((1, mf.shape[1]), jnp.float32)
    upper_mask = jnp.concatenate([mf[1:], zero_row], axis=0)
    row_ids = jnp.arange(mf.shape[0], dtype=jnp.int32)
    ey = jnp.where(row_ids[:, None] < mf.shape[0] - 1, coef_y * mf * upper_mask, 0.0)
    top_coef = coef_y[-1]
    top_mask = mf[-1]
    ef = 0.5 * (top_coef + top_coef[partner]) * top_mask * top_mask[partner]
    ex_left = jnp.roll(ex, 1, axis=1)
    ey_down = jnp.concatenate([zero_row, ey[:-1]], axis=0)
    field = gains * mf * values
    zero_rows = jnp.zeros((2, 1, mf.shape[1]), jnp.float32)
    for step in range(ITERS):
        scaled = inv_area * field
        right = jnp.roll(scaled, -1, axis=2)
        left = jnp.roll(scaled, 1, axis=2)
        upper = jnp.concatenate([scaled[:, 1:], zero_rows], axis=1)
        lower = jnp.concatenate([zero_rows, scaled[:, :-1]], axis=1)
        delta = ex * (right - scaled) + ex_left * (left - scaled) + ey * (upper - scaled) + ey_down * (lower - scaled)
        fold = ef * (scaled[:, -1][:, partner] - scaled[:, -1])
        delta = delta.at[:, -1].add(fold)
        field = field + delta
    return field


def reference(increment, normal_gain, coef_x, coef_y, ocean, inv_area, partner):
    inputs = (jnp.moveaxis(increment, 1, 0), jnp.moveaxis(normal_gain, 1, 0), coef_x, coef_y, ocean)
    result = lax.map(lambda item: level_adjoint(item, inv_area, partner), inputs)
    return jnp.moveaxis(result, 0, 1)
```

```python
import functools

import jax
import jax.numpy as jnp
from jax import lax
from jax.experimental import pallas as pl
from jax.experimental.pallas import tpu as pltpu
from jax.sharding import PartitionSpec as P

ITERS = 10
W = ITERS
LEV = 6
ROWS, COLS = 24, 512
NT = COLS // 128
RING = NT + 1
FIELDS = 4 * LEV + 1
KX, KY, AREA = 2 * LEV, 3 * LEV, 4 * LEV
PACKS = 3
M0 = 16
M1 = M0 + ROWS
HEIGHT = 56
SHARE = 3
MESH = pl.DeviceIdType.MESH
F32 = jnp.float32


def lanes_of(shape):
    return lax.broadcasted_iota(jnp.int32, shape, len(shape) - 1)


def east(tiles):
    lane = lanes_of(tiles[0].shape)
    turned = [pltpu.roll(t, 127, 1) for t in tiles]
    n = len(tiles)
    return [jnp.where(lane == 127, turned[(i + 1) % n], turned[i]) for i in range(n)]


def west(tiles):
    lane = lanes_of(tiles[0].shape)
    turned = [pltpu.roll(t, 1, 1) for t in tiles]
    n = len(tiles)
    return [jnp.where(lane == 0, turned[(i - 1) % n], turned[i]) for i in range(n)]


def slot(field):
    return field // 12, 10 * (field % 12)


def kernel(
    n_lat, n_lon,
    inc, gain, cx, cy, oc, ar, partner, out,
    inc_v, gain_v, cx_v, cy_v, oc_v, ar_v, part_s,
    D, H1, H2, EX, EY, O, P_, Q, F1, GG, F2,
    in_sem, out_sem, lat_s, lat_r, cor_s, cor_r, lon_s, lon_r,
    f1_s, f1_r, a1_s, a1_r, f2_s, f2_r,
):
    la, lo = lax.axis_index("lat"), lax.axis_index("lon")
    is_top, is_bottom = la == n_lat - 1, la == 0
    not_top, not_bottom = la < n_lat - 1, la > 0
    e_dev, w_dev = (la, lax.rem(lo + 1, n_lon)), (la, lax.rem(lo + n_lon - 1, n_lon))
    n_dev, s_dev = (la + 1, lo), (la - 1, lo)

    def mirror_dev(d):
        return lax.rem(lo + d, n_lon)

    bar = pltpu.get_barrier_semaphore()

    def greet(dev):
        pl.semaphore_signal(bar, inc=1, device_id=dev, device_id_type=MESH)

    greet(e_dev)
    greet(w_dev)

    @pl.when(not_top)
    def _():
        greet(n_dev)

    @pl.when(not_bottom)
    def _():
        greet(s_dev)

    @pl.when(is_top)
    def _():
        for d in range(2, n_lon - 1):
            greet((la, mirror_dev(d)))

    loads = [
        pltpu.make_async_copy(src, dst, in_sem.at[i])
        for i, (src, dst) in enumerate(
            [(oc, oc_v), (ar, ar_v), (cx, cx_v), (cy, cy_v), (gain, gain_v), (inc, inc_v),
             (partner.at[pl.ds(0, 1024)], part_s)]
        )
    ]
    for c in loads:
        c.start()
    for c in loads:
        c.wait()

    for ct in range(NT):
        for r in range(0, ROWS, 8):
            D[AREA, ct, pl.ds(M0 + r, 8), :] = ar_v[pl.ds(r, 8), pl.ds(ct * 128, 128)]

    def prepare(l, _):
        for ct in range(NT):
            cols = pl.ds(ct * 128, 128)
            for r in range(0, ROWS, 8):
                rows, own = pl.ds(r, 8), pl.ds(M0 + r, 8)
                m = oc_v[l, rows, cols].astype(F32)
                am = ar_v[rows, cols] * m
                D[KX + l, ct, own, :] = cx_v[l, rows, cols] * m
                D[KY + l, ct, own, :] = cy_v[l, rows, cols] * m
                for t in range(2):
                    D[t * LEV + l, ct, own, :] = am * (gain_v[t, l, rows, cols] * inc_v[t, l, rows, cols])
        return 0

    lax.fori_loop(0, LEV, prepare, 0)

    lane8 = lanes_of((8, 128))

    def pack(i, _):
        r = pl.multiple_of(i * 8, 8)
        for p in range(PACKS):
            to_e = to_w = None
            for f in range(12 * p, min(12 * p + 12, FIELDS)):
                at = slot(f)[1]
                last = pltpu.roll(D[f, NT - 1, pl.ds(M0 + r, 8), :], (W + at) % 128, 1)
                first = D[f, 0, pl.ds(M0 + r, 8), :]
                if at:
                    first = pltpu.roll(first, at, 1)
                to_e = last if to_e is None else jnp.where(lane8 >= at, last, to_e)
                to_w = first if to_w is None else jnp.where(lane8 >= at, first, to_w)
            P_[0, p, pl.ds(r, 8), :] = to_e
            P_[1, p, pl.ds(r, 8), :] = to_w
        return 0

    lax.fori_loop(0, ROWS // 8, pack, 0)

    def remote(src, dst, ss, rs, dev):
        return pltpu.make_async_remote_copy(
            src_ref=src, dst_ref=dst, send_sem=ss, recv_sem=rs, device_id=dev, device_id_type=MESH
        )

    own_q = Q.at[0, :, pl.ds(M0, ROWS), :], Q.at[1, :, pl.ds(M0, ROWS), :]
    lon = [
        remote(P_.at[0], own_q[0], lon_s.at[0], lon_r.at[0], e_dev),
        remote(P_.at[1], own_q[1], lon_s.at[1], lon_r.at[1], w_dev),
    ]
    main = pl.ds(0, NT)
    low, high = pl.ds(M0, W), pl.ds(M1 - W, W)
    below, above = pl.ds(M0 - W, W), pl.ds(M1, W)
    north = remote(D.at[:, main, high, :], D.at[:, main, below, :], lat_s.at[0], lat_r.at[0], n_dev)
    south = remote(D.at[:, main, low, :], D.at[:, main, above, :], lat_s.at[1], lat_r.at[1], s_dev)
    cor_n = remote(Q.at[:, :, high, :], Q.at[:, :, below, :], cor_s.at[0], cor_r.at[0], n_dev)
    cor_s_ = remote(Q.at[:, :, low, :], Q.at[:, :, above, :], cor_s.at[1], cor_r.at[1], s_dev)

    def share1(d):
        peer = mirror_dev(d)
        dev = (la, peer)
        return (
            remote(D.at[pl.ds(SHARE * peer, SHARE), main, high, :],
                   F1.at[lo, pl.ds(0, SHARE), :, pl.ds(0, W), :], f1_s.at[d], f1_r.at[d], dev),
            remote(D.at[pl.ds(AREA, 1), main, high, :],
                   F1.at[lo, pl.ds(SHARE, 1), :, pl.ds(0, W), :], a1_s.at[d], a1_r.at[d], dev),
        )

    def share2(d):
        peer = mirror_dev(d)
        return remote(F2.at[peer, :, :, pl.ds(0, W), :],
                      D.at[pl.ds(SHARE * lo, SHARE), :, above, :], f2_s.at[d], f2_r.at[d], (la, peer))

    pl.semaphore_wait(bar, jnp.where(is_top, n_lon, jnp.where(is_bottom, 3, 4)))

    for c in lon:
        c.start()

    @pl.when(is_top)
    def _():
        for d in range(1, n_lon):
            for c in share1(d):
                c.start()

    @pl.when(not_top)
    def _():
        north.start()

    @pl.when(not_bottom)
    def _():
        south.start()

    @pl.when(is_top)
    def _():
        keep = [
            pltpu.make_async_copy(D.at[pl.ds(SHARE * lo, SHARE), main, high, :],
                                  F1.at[lo, pl.ds(0, SHARE), :, pl.ds(0, W), :], f1_s.at[0]),
            pltpu.make_async_copy(D.at[pl.ds(AREA, 1), main, high, :],
                                  F1.at[lo, pl.ds(SHARE, 1), :, pl.ds(0, W), :], a1_s.at[0]),
        ]
        for c in keep:
            c.start()
        for c in keep:
            c.wait()

    @pl.when(is_bottom)
    def _():
        def clear(f, _):
            for ct in range(RING):
                for r in (M0 - W, M0 - 8):
                    D[f, ct, pl.ds(r, 8), :] = jnp.zeros((8, 128), F32)
            return 0

        lax.fori_loop(0, FIELDS, clear, 0)

    def unpack(r):
        for p in range(PACKS):
            w_side, e_side = Q[0, p, pl.ds(r, 8), :], Q[1, p, pl.ds(r, 8), :]
            for f in range(12 * p, min(12 * p + 12, FIELDS)):
                at = slot(f)[1]
                wv = pltpu.roll(w_side, (128 - W - at) % 128, 1)
                ev = pltpu.roll(e_side, (128 - at) % 128, 1) if at else e_side
                D[f, NT, pl.ds(r, 8), :] = jnp.where(lane8 < 64, ev, wv)

    for c in lon:
        c.wait_recv()

    @pl.when(not_top)
    def _():
        cor_n.start()

    @pl.when(not_bottom)
    def _():
        cor_s_.start()

    def unpack_own(i, _):
        unpack(M0 + pl.multiple_of(i * 8, 8))
        return 0

    lax.fori_loop(0, ROWS // 8, unpack_own, 0)

    @pl.when(is_top)
    def _():
        for d in range(1, n_lon):
            for c in share1(d):
                c.wait_recv()
        pivot = part_s[0]
        cq, cr = pivot // 128, lax.rem(pivot, 128)
        lane_from = (cr - lane8) & 127
        row_from = 7 - lax.broadcasted_iota(jnp.int32, (8, 128), 0)

        def flip(x):
            return jnp.take_along_axis(jnp.take_along_axis(x, row_from, axis=0), lane_from, axis=1)

        def turn(s, _):
            for ct in range(NT):
                for f in range(SHARE + 1):
                    GG[s * NT + ct, f, pl.ds(0, 8), :] = flip(F1[s, f, ct, pl.ds(2, 8), :])
                    GG[s * NT + ct, f, pl.ds(2, 8), :] = flip(F1[s, f, ct, pl.ds(0, 8), :])
            return 0

        lax.fori_loop(0, n_lon, turn, 0)
        lane16 = lanes_of((16, 128))
        tiles = n_lon * NT

        def image(m, ct, f):
            at = (cq - NT * m - ct + 2 * tiles) % tiles
            return jnp.where(lane16 <= cr, GG[at, f], GG[(at + tiles - 1) % tiles, f])

        def ring_image(m, ct, f):
            if ct < NT:
                return image(m, ct, f)
            return jnp.where(lane16 < 64, image(m, NT, f), image(m, -1, f))

        def send_image(m, _):
            for f in range(SHARE):
                for ct in range(RING):
                    F2[m, f, ct] = ring_image(m, ct, f)
            return 0

        lax.fori_loop(0, n_lon, send_image, 0)
        for d in range(1, n_lon):
            share2(d).start()
        keep = pltpu.make_async_copy(F2.at[lo, :, :, pl.ds(0, W), :],
                                     D.at[pl.ds(SHARE * lo, SHARE), :, above, :], f2_s.at[0])
        keep.start()
        for ct in range(RING):
            D[AREA, ct, above, :] = ring_image(lo, ct, SHARE)[:W]
        keep.wait()

    @pl.when(not_bottom)
    def _():
        cor_n.wait_recv()
        for r in (M0 - W, M0 - 8):
            unpack(r)
        north.wait_recv()

    @pl.when(not_top)
    def _():
        cor_s_.wait_recv()
        for r in (M1, M1 + W - 8):
            unpack(r)
        south.wait_recv()

    @pl.when(is_top)
    def _():
        for d in range(1, n_lon):
            share2(d).wait_recv()

    def wet(x):
        return jnp.where(x != 0.0, 1.0, 0.0).astype(F32)

    def faces(l, _):
        for r in range(M0 - W, M1 + W, 8):
            rows, upper = pl.ds(r, 8), pl.ds(r + 1, 8)
            kx = [D[KX + l, ct, rows, :] for ct in range(RING)]
            for ct, me in enumerate(east([wet(x) for x in kx])):
                EX[l, ct, rows, :] = kx[ct] * me
                EY[l, ct, rows, :] = D[KY + l, ct, rows, :] * wet(D[KX + l, ct, upper, :])
        return 0

    lax.fori_loop(0, LEV, faces, 0)

    @pl.when(is_top)
    def _():
        def fold_faces(l, _):
            for r in (M1, M1 + W - 8):
                rows, upper = pl.ds(r, 8), pl.ds(r + 1, 8)
                kx = [D[KX + l, ct, rows, :] for ct in range(RING)]
                for ct, xe in enumerate(east(kx)):
                    m = wet(kx[ct])
                    EX[l, ct, rows, :] = xe * m
                    EY[l, ct, rows, :] = D[KY + l, ct, upper, :] * m
            here, there = pl.ds(M1 - 1, 1), pl.ds(M1, 1)
            for ct in range(RING):
                EY[l, ct, here, :] = 0.5 * (
                    D[KY + l, ct, here, :] * wet(D[KX + l, ct, there, :])
                    + D[KY + l, ct, there, :] * wet(D[KX + l, ct, here, :])
                )
            return 0

        lax.fori_loop(0, LEV, fold_faces, 0)

    def steps(k, src, dst):
        lower = M0 - W + k
        count = -(-(ROWS + 2 * (W - k)) // 8)

        def level(l, _):
            for i in range(count):
                r = lower + 8 * i
                rows, up, down = pl.ds(r, 8), pl.ds(r + 1, 8), pl.ds(r - 1, 8)
                ex = [EX[l, ct, rows, :] for ct in range(RING)]
                for t in range(2):
                    f = t * LEV + l
                    h = [src[f, ct, rows, :] for ct in range(RING)]
                    fx = [e * (he - hc) for e, he, hc in zip(ex, east(h), h)]
                    fw = west(fx)
                    for ct in range(RING if k < W else NT):
                        d = (fx[ct] - fw[ct]) + (
                            EY[l, ct, rows, :] * (src[f, ct, up, :] - h[ct])
                            - EY[l, ct, down, :] * (h[ct] - src[f, ct, down, :])
                        )
                        a = D[AREA, ct, rows, :]
                        if k < W:
                            dst[f, ct, rows, :] = h[ct] + a * d
                        else:
                            O[t, l, pl.ds(r - M0, 8), pl.ds(ct * 128, 128)] = h[ct] / a + d
            if k == W:
                for t in range(2):
                    pltpu.make_async_copy(O.at[t, l], out.at[t, l], out_sem.at[t, l]).start()
            return 0

        lax.fori_loop(0, LEV, level, 0)

    src, spare = D, (H1, H2)
    for k in range(1, W + 1):
        dst = spare[k % 2]
        steps(k, src, dst)
        src = dst

    for c in lon:
        c.wait_send()

    @pl.when(not_top)
    def _():
        north.wait_send()
        cor_n.wait_send()

    @pl.when(not_bottom)
    def _():
        south.wait_send()
        cor_s_.wait_send()

    @pl.when(is_top)
    def _():
        for d in range(1, n_lon):
            for c in share1(d):
                c.wait_send()
            share2(d).wait_send()

    for t in range(2):
        for l in range(LEV):
            pltpu.make_async_copy(O.at[t, l], out.at[t, l], out_sem.at[t, l]).wait()


def on_device(n_lat, n_lon, *args):
    vmem = lambda *shape: pltpu.VMEM(shape, F32)
    dma = lambda *shape: pltpu.SemaphoreType.DMA(shape)
    scratch = [
        vmem(2, LEV, ROWS, COLS), vmem(2, LEV, ROWS, COLS), vmem(LEV, ROWS, COLS), vmem(LEV, ROWS, COLS),
        pltpu.VMEM((LEV, ROWS, COLS), jnp.int32), vmem(ROWS, COLS), pltpu.SMEM((1024,), jnp.int32),
        vmem(FIELDS, RING, HEIGHT, 128), vmem(2 * LEV, RING, HEIGHT, 128), vmem(2 * LEV, RING, HEIGHT, 128),
        vmem(LEV, RING, HEIGHT, 128), vmem(LEV, RING, HEIGHT, 128), vmem(2, LEV, ROWS, COLS),
        vmem(2, PACKS, ROWS, 128), vmem(2, PACKS, HEIGHT, 128),
        vmem(n_lon, SHARE + 1, NT, 16, 128), vmem(n_lon * NT, SHARE + 1, 16, 128),
        vmem(n_lon, SHARE, RING, 16, 128),
        dma(7), dma(2, LEV), dma(2), dma(2), dma(2), dma(2), dma(2), dma(2),
        dma(n_lon), dma(n_lon), dma(n_lon), dma(n_lon), dma(n_lon), dma(n_lon),
    ]
    return pl.pallas_call(
        functools.partial(kernel, n_lat, n_lon),
        out_shape=jax.ShapeDtypeStruct((2, LEV, ROWS, COLS), F32),
        in_specs=[pl.BlockSpec(memory_space=pl.ANY)] * 7,
        out_specs=pl.BlockSpec(memory_space=pl.ANY),
        scratch_shapes=scratch,
        compiler_params=pltpu.CompilerParams(
            collective_id=0, has_side_effects=True, vmem_limit_bytes=40 * 2**20
        ),
    )(*args)


def solution(mesh):
    in_specs = (
        P(None, None, "lat", "lon"),
        P(None, None, "lat", "lon"),
        P(None, "lat", "lon"),
        P(None, "lat", "lon"),
        P(None, "lat", "lon"),
        P("lat", "lon"),
        P(),
    )
    out_specs = P(None, None, "lat", "lon")
    return jax.shard_map(
        functools.partial(on_device, mesh.shape["lat"], mesh.shape["lon"]),
        mesh=mesh, in_specs=in_specs, out_specs=out_specs, check_vma=False,
    )
```

```python
import functools
import itertools

import jax
import jax.numpy as jnp
from jax import lax
from jax.experimental import pallas as pl
from jax.experimental.pallas import tpu as pltpu
from jax.sharding import PartitionSpec as P

ITERS = 10
W = ITERS
LEV = 6
ROWS, COLS = 24, 512
NT = COLS // 128
RING = NT + 1
FIELDS = 4 * LEV + 1
KX, KY, AREA = 2 * LEV, 3 * LEV, 4 * LEV
PACKS = 3
M0 = 16
M1 = M0 + ROWS
HEIGHT = 56
GROUP = 128 // NT
LEVELS_AT_ONCE = 3
SHARE = 3
MESH = pl.DeviceIdType.MESH
F32 = jnp.float32


def lanes_of(shape):
    return lax.broadcasted_iota(jnp.int32, shape, len(shape) - 1)


def pick(choices, by):
    out = choices[-1]
    for i in range(len(choices) - 2, -1, -1):
        out = jnp.where(by == i, choices[i], out)
    return out


def take(x, lanes):
    return jnp.take_along_axis(x, lanes, axis=1)


def interleave(tiles):
    lane = lanes_of(tiles[0].shape)
    group, place = lane // GROUP, lane % GROUP
    sorted_ = [take(x, NT * place + (group - j + NT) % NT) for j, x in enumerate(tiles)]
    mixed = [pick([sorted_[(g - c) % NT] for g in range(NT)], group) for c in range(NT)]
    return [pltpu.roll(x, (128 - GROUP * c) % 128, 1) if c else x for c, x in enumerate(mixed)]


def in_order(tiles):
    lane = lanes_of(tiles[0].shape)
    group = lane // GROUP
    mixed = [pltpu.roll(x, GROUP * c, 1) if c else x for c, x in enumerate(tiles)]
    sorted_ = [pick([mixed[(g - j) % NT] for g in range(NT)], group) for j in range(NT)]
    return [take(x, GROUP * ((lane % NT + j) % NT) + lane // NT) for j, x in enumerate(sorted_)]


def east(x):
    last = lanes_of(x[0].shape) == 127
    main, halo = pltpu.roll(x[0], 127, 1), pltpu.roll(x[NT], 127, 1)
    return x[1:NT] + [jnp.where(last, halo, main), jnp.where(last, main, halo)]


def west(x):
    first = lanes_of(x[0].shape) == 0
    main, halo = pltpu.roll(x[NT - 1], 1, 1), pltpu.roll(x[NT], 1, 1)
    return [jnp.where(first, halo, main)] + x[: NT - 1] + [jnp.where(first, main, halo)]


def slot(field):
    return field // 12, 10 * (field % 12)


def wet(masked):
    return jnp.where(masked != 0.0, 1.0, 0.0).astype(F32)


def inner_rows(k):
    n = ROWS - 2 * k
    if n < 8:
        return [M0 + ROWS // 2 - 4]
    chunks = [M0 + k + 8 * j for j in range(n // 8)]
    return chunks + [M1 - k - 8] if n % 8 else chunks


def kernel(
    n_lat, n_lon,
    inc, gain, cx, cy, oc, ar, partner, out,
    inc_v, gain_v, cx_v, cy_v, oc_v, ar_v, part_s,
    D, H1, H2, H3, H4, H5, H6, H7, H8, H9, C0, CE, CW, CN, CS, RA, O, EDGE, P_, Q, F1, GG, F2,
    in_sem, out_sem, lat_s, lat_r, cor_s, cor_r, lon_s, lon_r, f1_s, f1_r, f2_s, f2_r,
):
    la, lo = lax.axis_index("lat"), lax.axis_index("lon")
    is_top, is_bottom = la == n_lat - 1, la == 0
    not_top, not_bottom = la < n_lat - 1, la > 0
    e_dev, w_dev = (la, lax.rem(lo + 1, n_lon)), (la, lax.rem(lo + n_lon - 1, n_lon))
    n_dev, s_dev = (la + 1, lo), (la - 1, lo)

    def mirror_dev(d):
        return lax.rem(lo + d, n_lon)

    bar = pltpu.get_barrier_semaphore()

    def greet(dev):
        pl.semaphore_signal(bar, inc=1, device_id=dev, device_id_type=MESH)

    greet(e_dev)
    greet(w_dev)

    @pl.when(not_top)
    def _():
        greet(n_dev)

    @pl.when(not_bottom)
    def _():
        greet(s_dev)

    @pl.when(is_top)
    def _():
        for d in range(2, n_lon - 1):
            greet((la, mirror_dev(d)))

    loads = [
        pltpu.make_async_copy(src, dst, in_sem.at[i])
        for i, (src, dst) in enumerate(
            [(oc, oc_v), (ar, ar_v), (cx, cx_v), (cy, cy_v), (gain, gain_v), (inc, inc_v),
             (partner.at[pl.ds(0, 1024)], part_s)]
        )
    ]
    for c in loads:
        c.start()
    def place(field, r, tiles):
        EDGE[field, 0, pl.ds(r, 8), :] = tiles[0]
        EDGE[field, 1, pl.ds(r, 8), :] = tiles[NT - 1]
        for c, x in enumerate(interleave(tiles)):
            D[field, c, pl.ds(M0 + r, 8), :] = x

    runs = [pl.ds(j * 128, 128) for j in range(NT)]

    def faces(i, _):
        for l in (2 * i, 2 * i + 1):
            for r in range(0, ROWS, 8):
                rows = pl.ds(r, 8)
                m = [oc_v[l, rows, j].astype(F32) for j in runs]
                place(KX + l, r, [cx_v[l, rows, j] * mj for j, mj in zip(runs, m)])
                place(KY + l, r, [cy_v[l, rows, j] * mj for j, mj in zip(runs, m)])
        return 0

    def cells(i, _):
        for l in (2 * i, 2 * i + 1):
            for r in range(0, ROWS, 8):
                rows = pl.ds(r, 8)
                am = [ar_v[rows, j] * oc_v[l, rows, j].astype(F32) for j in runs]
                for t in range(2):
                    place(t * LEV + l, r,
                          [x * (gain_v[t, l, rows, j] * inc_v[t, l, rows, j]) for j, x in zip(runs, am)])
        return 0

    for c in loads[:4]:
        c.wait()
    for r in range(0, ROWS, 8):
        place(AREA, r, [ar_v[pl.ds(r, 8), j] for j in runs])
    lax.fori_loop(0, LEV // 2, faces, 0)
    for c in loads[4:]:
        c.wait()
    lax.fori_loop(0, LEV // 2, cells, 0)

    lane8 = lanes_of((8, 128))

    def pack(i, _):
        rows = pl.ds(pl.multiple_of(i * 8, 8), 8)
        for p in range(PACKS):
            to_e = to_w = None
            for f in range(12 * p, min(12 * p + 12, FIELDS)):
                at = slot(f)[1]
                last = pltpu.roll(EDGE[f, 1, rows, :], (W + at) % 128, 1)
                first = EDGE[f, 0, rows, :]
                if at:
                    first = pltpu.roll(first, at, 1)
                to_e = last if to_e is None else jnp.where(lane8 >= at, last, to_e)
                to_w = first if to_w is None else jnp.where(lane8 >= at, first, to_w)
            P_[0, p, rows, :] = to_e
            P_[1, p, rows, :] = to_w
        return 0


    def remote(src, dst, ss, rs, dev):
        return pltpu.make_async_remote_copy(
            src_ref=src, dst_ref=dst, send_sem=ss, recv_sem=rs, device_id=dev, device_id_type=MESH
        )

    own_q = Q.at[0, :, pl.ds(M0, ROWS), :], Q.at[1, :, pl.ds(M0, ROWS), :]
    lon = [
        remote(P_.at[0], own_q[0], lon_s.at[0], lon_r.at[0], e_dev),
        remote(P_.at[1], own_q[1], lon_s.at[1], lon_r.at[1], w_dev),
    ]
    main = pl.ds(0, NT)
    low, high = pl.ds(M0, W), pl.ds(M1 - W, W)
    below, above = pl.ds(M0 - W, W), pl.ds(M1, W)
    north = remote(D.at[:, main, high, :], D.at[:, main, below, :], lat_s.at[0], lat_r.at[0], n_dev)
    south = remote(D.at[:, main, low, :], D.at[:, main, above, :], lat_s.at[1], lat_r.at[1], s_dev)
    cor_n = remote(Q.at[:, :, high, :], Q.at[:, :, below, :], cor_s.at[0], cor_r.at[0], n_dev)
    cor_s_ = remote(Q.at[:, :, low, :], Q.at[:, :, above, :], cor_s.at[1], cor_r.at[1], s_dev)

    def share1(f, d):
        peer = mirror_dev(d)
        field = AREA if f == SHARE else SHARE * peer + f
        return remote(D.at[pl.ds(field, 1), main, high, :], F1.at[lo, pl.ds(f, 1), :, pl.ds(0, W), :],
                      f1_s.at[f, d], f1_r.at[f, d], (la, peer))

    def share2(f, d):
        peer = mirror_dev(d)
        return remote(F2.at[peer, pl.ds(f, 1), :, pl.ds(0, W), :], D.at[pl.ds(SHARE * lo + f, 1), :, above, :],
                      f2_s.at[f, d], f2_r.at[f, d], (la, peer))

    lax.fori_loop(0, ROWS // 8, pack, 0)

    pl.semaphore_wait(bar, jnp.where(is_top, n_lon, jnp.where(is_bottom, 3, 4)))

    for c in lon:
        c.start()

    @pl.when(is_top)
    def _():
        for f in range(SHARE + 1):
            for d in range(1, n_lon):
                share1(f, d).start()

    @pl.when(not_top)
    def _():
        north.start()

    @pl.when(not_bottom)
    def _():
        south.start()

    @pl.when(is_top)
    def _():
        keep = [
            pltpu.make_async_copy(D.at[pl.ds(SHARE * lo, SHARE), main, high, :],
                                  F1.at[lo, pl.ds(0, SHARE), :, pl.ds(0, W), :], f1_s.at[0, 0]),
            pltpu.make_async_copy(D.at[pl.ds(AREA, 1), main, high, :],
                                  F1.at[lo, pl.ds(SHARE, 1), :, pl.ds(0, W), :], f1_s.at[1, 0]),
        ]
        for c in keep:
            c.start()
        for c in keep:
            c.wait()

    @pl.when(is_bottom)
    def _():
        def clear(f, _):
            for ct in range(RING):
                for r in (M0 - W, M0 - 8):
                    D[f, ct, pl.ds(r, 8), :] = jnp.zeros((8, 128), F32)
            return 0

        lax.fori_loop(0, FIELDS, clear, 0)

    for c in range(NT):
        for r in range(M0, M1, 8):
            RA[c, pl.ds(r, 8), :] = 1.0 / D[AREA, c, pl.ds(r, 8), :]

    def unpack(r):
        for p in range(PACKS):
            w_side, e_side = Q[0, p, pl.ds(r, 8), :], Q[1, p, pl.ds(r, 8), :]
            for f in range(12 * p, min(12 * p + 12, FIELDS)):
                at = slot(f)[1]
                wv = pltpu.roll(w_side, (128 - W - at) % 128, 1)
                ev = pltpu.roll(e_side, (128 - at) % 128, 1) if at else e_side
                D[f, NT, pl.ds(r, 8), :] = jnp.where(lane8 < 64, ev, wv)

    def weights(chunks, fold):
        def levels(i, _):
            for l, r in itertools.product([LEVELS_AT_ONCE * i + q for q in range(LEVELS_AT_ONCE)], chunks):
                rows, up, down = pl.ds(r, 8), pl.ds(r + 1, 8), pl.ds(r - 1, 8)
                row = r + lax.broadcasted_iota(jnp.int32, (8, 128), 0)
                kx = [D[KX + l, ct, rows, :] for ct in range(RING)]
                m = [wet(x) for x in kx]
                ex = [k * n for k, n in zip(kx, east(m))]
                if fold:
                    ex = [jnp.where(row >= M1, k * n, x) for k, n, x in zip(east(kx), m, ex)]
                for ct, ew in enumerate(west(ex)):
                    ky, ky_s = D[KY + l, ct, rows, :], D[KY + l, ct, down, :]
                    m_n = wet(D[KX + l, ct, up, :])
                    yn, ys = ky * m_n, ky_s * m[ct]
                    if fold:
                        ky_n, m_s = D[KY + l, ct, up, :], wet(D[KX + l, ct, down, :])
                        yn_f, ys_f = ky_n * m[ct], ky * m_s
                        yn = jnp.where(row >= M1, yn_f, jnp.where(row == M1 - 1, 0.5 * (yn + yn_f), yn))
                        ys = jnp.where(row > M1, ys_f, jnp.where(row == M1, 0.5 * (ys + ys_f), ys))
                    a = D[AREA, ct, rows, :]
                    ce, cw, cn, cs = a * ex[ct], a * ew, a * yn, a * ys
                    CE[l, ct, rows, :], CW[l, ct, rows, :] = ce, cw
                    CN[l, ct, rows, :], CS[l, ct, rows, :] = cn, cs
                    C0[l, ct, rows, :] = 1.0 - ((ce + cw) + (cn + cs))
            return 0

        lax.fori_loop(0, LEV // LEVELS_AT_ONCE, levels, 0)

    H = (D, H1, H2, H3, H4, H5, H6, H7, H8, H9)

    def advance(k, chunks):
        src = H[k - 1]

        def levels(i, _):
            for q in range(LEVELS_AT_ONCE):
                l = LEVELS_AT_ONCE * i + q
                for r in chunks:
                    rows, up, down = pl.ds(r, 8), pl.ds(r + 1, 8), pl.ds(r - 1, 8)
                    cs = [[C[l, ct, rows, :] for C in (C0, CE, CW, CN, CS)] for ct in range(RING)]
                    for t in range(2):
                        f = t * LEV + l
                        h = [src[f, ct, rows, :] for ct in range(RING)]
                        he, hw = east(h), west(h)
                        new = []
                        for ct in range(RING if k < ITERS else NT):
                            c0, ce, cw, cn, c_s = cs[ct]
                            new.append((c0 * h[ct] + ce * he[ct]) + (
                                cw * hw[ct] + (cn * src[f, ct, up, :] + c_s * src[f, ct, down, :])))
                        if k < ITERS:
                            for ct in range(RING):
                                H[k][f, ct, rows, :] = new[ct]
                        else:
                            g = in_order([x * RA[ct, rows, :] for ct, x in enumerate(new)])
                            for j in range(NT):
                                O[t, l, j, pl.ds(r - M0, 8), :] = g[j]
            return 0

        lax.fori_loop(0, LEV // LEVELS_AT_ONCE, levels, 0)

    for c in lon:
        c.wait_recv()

    @pl.when(not_top)
    def _():
        cor_n.start()

    @pl.when(not_bottom)
    def _():
        cor_s_.start()

    def unpack_own(i, _):
        unpack(M0 + pl.multiple_of(i * 8, 8))
        return 0

    lax.fori_loop(0, ROWS // 8, unpack_own, 0)
    weights(inner_rows(1), False)

    @pl.when(is_top)
    def _():
        pivot = part_s[0] + n_lon * COLS
        row_from = 7 - lax.broadcasted_iota(jnp.int32, (8, 128), 0)
        lane16 = lanes_of((16, 128))

        def counterpart(c):
            other = lax.rem(pivot - c, NT)
            at = (pivot - c - other) // NT
            return other, at // 128, lax.rem(at, 128)

        def turn(f):
            for s, c in itertools.product(range(n_lon), range(NT)):
                lanes = (counterpart(c)[2] - lane8) & 127
                for to, start in ((0, 2), (2, 0)):
                    x = jnp.take_along_axis(F1[s, f, c, pl.ds(start, 8), :], row_from, axis=0)
                    GG[f, s, c, pl.ds(to, 8), :] = take(x, lanes)

        def image(m, c, f):
            other, at, lane = counterpart(c)
            block = lax.rem(at - m + 2 * n_lon, n_lon)
            return jnp.where(lane16 <= lane, GG[f, block, other],
                             GG[f, lax.rem(block + n_lon - 1, n_lon), other])

        def halo(eastern, western):
            both = [jnp.where(lane16 < 64, e, w) for e, w in zip(eastern, western)]
            lanes = lane16 // NT + jnp.where(lane16 < 64, 0, 128 - GROUP)
            return pick([take(x, lanes) for x in both], lane16 % NT)

        for f in range(SHARE):
            for d in range(1, n_lon):
                share1(f, d).wait_recv()
            turn(f)

            for m, c in itertools.product(range(n_lon), range(NT)):
                F2[m, f, c] = image(m, c, f)
            for m in range(n_lon):
                e, w = (m + 1) % n_lon, (m - 1) % n_lon
                F2[m, f, NT] = halo([F2[e, f, c] for c in range(NT)], [F2[w, f, c] for c in range(NT)])
            for d in range(1, n_lon):
                share2(f, d).start()
        for d in range(1, n_lon):
            share1(SHARE, d).wait_recv()
        turn(SHARE)
        for c in range(NT):
            D[AREA, c, above, :] = image(lo, c, SHARE)[:W]
        e, w = lax.rem(lo + 1, n_lon), lax.rem(lo + n_lon - 1, n_lon)
        D[AREA, NT, above, :] = halo([image(e, c, SHARE) for c in range(NT)],
                                     [image(w, c, SHARE) for c in range(NT)])[:W]
        keep = pltpu.make_async_copy(F2.at[lo, :, :, pl.ds(0, W), :],
                                     D.at[pl.ds(SHARE * lo, SHARE), :, above, :], f2_s.at[0, 0])
        keep.start()
        keep.wait()

    for k in range(1, ITERS + 1):
        advance(k, inner_rows(k))

    def side(i, _):
        northern = i == lax.rem(la, 2)
        southern = i != lax.rem(la, 2)

        @pl.when(southern & not_bottom)
        def _():
            cor_n.wait_recv()
            for r in (M0 - W, M0 - 8):
                unpack(r)
            north.wait_recv()

        @pl.when(southern)
        def _():
            weights((M0 - W + 1, M0 - 7), False)

        @pl.when(northern & not_top)
        def _():
            cor_s_.wait_recv()
            for r in (M1, M1 + W - 8):
                unpack(r)
            south.wait_recv()
            weights((M1 - 1, M1 + W - 9), False)

        @pl.when(northern & is_top)
        def _():
            for f in range(SHARE):
                for d in range(1, n_lon):
                    share2(f, d).wait_recv()
            weights((M1 - 1, M1 + W - 9), True)

        @pl.when(southern)
        def _():
            for k in range(1, ITERS + 1):
                advance(k, (M0 - W + k, M0 - 8 + k))

        @pl.when(northern)
        def _():
            for k in range(1, ITERS + 1):
                advance(k, (M1 - k, M1 + W - 8 - k))

        return 0

    lax.fori_loop(0, 2, side, 0)
    results = [
        pltpu.make_async_copy(O.at[:, :, j], out.at[:, :, :, pl.ds(128 * j, 128)], out_sem.at[j])
        for j in range(NT)
    ]
    for c in results:
        c.start()

    for c in lon:
        c.wait_send()

    @pl.when(not_top)
    def _():
        north.wait_send()
        cor_n.wait_send()

    @pl.when(not_bottom)
    def _():
        south.wait_send()
        cor_s_.wait_send()

    @pl.when(is_top)
    def _():
        for d in range(1, n_lon):
            for f in range(SHARE + 1):
                share1(f, d).wait_send()
            for f in range(SHARE):
                share2(f, d).wait_send()

    for c in results:
        c.wait()


def on_device(n_lat, n_lon, *args):
    vmem = lambda *shape: pltpu.VMEM(shape, F32)
    dma = lambda *shape: pltpu.SemaphoreType.DMA(shape)
    scratch = [
        vmem(2, LEV, ROWS, COLS), vmem(2, LEV, ROWS, COLS), vmem(LEV, ROWS, COLS), vmem(LEV, ROWS, COLS),
        pltpu.VMEM((LEV, ROWS, COLS), jnp.int32), vmem(ROWS, COLS), pltpu.SMEM((1024,), jnp.int32),
        vmem(FIELDS, RING, HEIGHT, 128), *[vmem(2 * LEV, RING, HEIGHT, 128)] * (ITERS - 1),
        *[vmem(LEV, RING, HEIGHT, 128)] * 5, vmem(NT, HEIGHT, 128), vmem(2, LEV, NT, ROWS, 128),
        vmem(FIELDS, 2, ROWS, 128), vmem(2, PACKS, ROWS, 128), vmem(2, PACKS, HEIGHT, 128),
        vmem(n_lon, SHARE + 1, NT, 16, 128), vmem(SHARE + 1, n_lon, NT, 16, 128),
        vmem(n_lon, SHARE, RING, 16, 128),
        dma(7), dma(NT), dma(2), dma(2), dma(2), dma(2), dma(2), dma(2),
        dma(SHARE + 1, n_lon), dma(SHARE + 1, n_lon), dma(SHARE, n_lon), dma(SHARE, n_lon),
    ]
    return pl.pallas_call(
        functools.partial(kernel, n_lat, n_lon),
        out_shape=jax.ShapeDtypeStruct((2, LEV, ROWS, COLS), F32),
        in_specs=[pl.BlockSpec(memory_space=pl.ANY)] * 7,
        out_specs=pl.BlockSpec(memory_space=pl.ANY),
        scratch_shapes=scratch,
        compiler_params=pltpu.CompilerParams(
            collective_id=0, has_side_effects=True, vmem_limit_bytes=60 * 2**20
        ),
    )(*args)


def solution(mesh):
    in_specs = (
        P(None, None, "lat", "lon"),
        P(None, None, "lat", "lon"),
        P(None, "lat", "lon"),
        P(None, "lat", "lon"),
        P(None, "lat", "lon"),
        P("lat", "lon"),
        P(),
    )
    out_specs = P(None, None, "lat", "lon")
    return jax.shard_map(
        functools.partial(on_device, mesh.shape["lat"], mesh.shape["lon"]),
        mesh=mesh, in_specs=in_specs, out_specs=out_specs, check_vma=False,
    )
```

```python
import functools
import itertools

import jax
import jax.numpy as jnp
from jax import lax
from jax.experimental import pallas as pl
from jax.experimental.pallas import tpu as pltpu
from jax.sharding import PartitionSpec as P

ITERS = 10
W = ITERS
LEV = 6
ROWS, COLS = 24, 512
NT = COLS // 128
RING = NT + 1
FIELDS = 4 * LEV + 1
KX, KY, AREA = 2 * LEV, 3 * LEV, 4 * LEV
PACKS = 3
M0 = 16
M1 = M0 + ROWS
HEIGHT = 56
GROUP = 128 // NT
LEVELS_AT_ONCE = 3
SHARE = 3
MESH = pl.DeviceIdType.MESH
F32 = jnp.float32


def lanes_of(shape):
    return lax.broadcasted_iota(jnp.int32, shape, len(shape) - 1)


def pick(choices, by):
    out = choices[-1]
    for i in range(len(choices) - 2, -1, -1):
        out = jnp.where(by == i, choices[i], out)
    return out


def take(x, lanes):
    return jnp.take_along_axis(x, lanes, axis=1)


def interleave(tiles):
    lane = lanes_of(tiles[0].shape)
    group, place = lane // GROUP, lane % GROUP
    sorted_ = [take(x, NT * place + (group - j + NT) % NT) for j, x in enumerate(tiles)]
    mixed = [pick([sorted_[(g - c) % NT] for g in range(NT)], group) for c in range(NT)]
    return [pltpu.roll(x, (128 - GROUP * c) % 128, 1) if c else x for c, x in enumerate(mixed)]


def in_order(tiles):
    lane = lanes_of(tiles[0].shape)
    group = lane // GROUP
    mixed = [pltpu.roll(x, GROUP * c, 1) if c else x for c, x in enumerate(tiles)]
    sorted_ = [pick([mixed[(g - j) % NT] for g in range(NT)], group) for j in range(NT)]
    return [take(x, GROUP * ((lane % NT + j) % NT) + lane // NT) for j, x in enumerate(sorted_)]


def east(x):
    last = lanes_of(x[0].shape) == 127
    main, halo = pltpu.roll(x[0], 127, 1), pltpu.roll(x[NT], 127, 1)
    return x[1:NT] + [jnp.where(last, halo, main), jnp.where(last, main, halo)]


def west(x):
    first = lanes_of(x[0].shape) == 0
    main, halo = pltpu.roll(x[NT - 1], 1, 1), pltpu.roll(x[NT], 1, 1)
    return [jnp.where(first, halo, main)] + x[: NT - 1] + [jnp.where(first, main, halo)]


def slot(field):
    return field // 12, 10 * (field % 12)


def wet(masked):
    return jnp.where(masked != 0.0, 1.0, 0.0).astype(F32)


def inner_rows(k):
    n = ROWS - 2 * k
    if n < 8:
        return [M0 + ROWS // 2 - 4]
    chunks = [M0 + k + 8 * j for j in range(n // 8)]
    return chunks + [M1 - k - 8] if n % 8 else chunks


def kernel(
    n_lat, n_lon,
    inc, gain, cx, cy, oc, ar, partner, out,
    inc_v, gain_v, cx_v, cy_v, oc_v, ar_v, part_s,
    D, H1, H2, H3, H4, H5, H6, H7, H8, H9, C0, CE, CW, CN, CS, RA, O, EDGE, P_, Q, F1, GG, F2,
    in_sem, out_sem, lat_s, lat_r, cor_s, cor_r, lon_s, lon_r, f1_s, f1_r, f2_s, f2_r,
):
    la, lo = lax.axis_index("lat"), lax.axis_index("lon")
    is_top, is_bottom = la == n_lat - 1, la == 0
    not_top, not_bottom = la < n_lat - 1, la > 0
    e_dev, w_dev = (la, lax.rem(lo + 1, n_lon)), (la, lax.rem(lo + n_lon - 1, n_lon))
    n_dev, s_dev = (la + 1, lo), (la - 1, lo)

    def mirror_dev(d):
        return lax.rem(lo + d, n_lon)

    bar = pltpu.get_barrier_semaphore()

    def greet(dev):
        pl.semaphore_signal(bar, inc=1, device_id=dev, device_id_type=MESH)

    greet(e_dev)
    greet(w_dev)

    @pl.when(not_top)
    def _():
        greet(n_dev)

    @pl.when(not_bottom)
    def _():
        greet(s_dev)

    @pl.when(is_top)
    def _():
        for d in range(2, n_lon - 1):
            greet((la, mirror_dev(d)))

    loads = [
        pltpu.make_async_copy(src, dst, in_sem.at[i])
        for i, (src, dst) in enumerate(
            [(oc, oc_v), (ar, ar_v), (cx, cx_v), (cy, cy_v), (gain, gain_v), (inc, inc_v),
             (partner.at[pl.ds(0, 1024)], part_s)]
        )
    ]
    for c in loads:
        c.start()
    def edges(field, r, tiles):
        EDGE[field, 0, pl.ds(r, 8), :] = tiles[0]
        EDGE[field, 1, pl.ds(r, 8), :] = tiles[-1]

    def place(field, r, tiles):
        for c, x in enumerate(interleave(tiles)):
            D[field, c, pl.ds(M0 + r, 8), :] = x

    runs = [pl.ds(j * 128, 128) for j in range(NT)]

    def faces(put, runs, l):
        for r in range(0, ROWS, 8):
            rows = pl.ds(r, 8)
            m = [oc_v[l, rows, j].astype(F32) for j in runs]
            put(KX + l, r, [cx_v[l, rows, j] * mj for j, mj in zip(runs, m)])
            put(KY + l, r, [cy_v[l, rows, j] * mj for j, mj in zip(runs, m)])

    def cells(put, runs, l):
        for r in range(0, ROWS, 8):
            rows = pl.ds(r, 8)
            am = [ar_v[rows, j] * oc_v[l, rows, j].astype(F32) for j in runs]
            for t in range(2):
                put(t * LEV + l, r,
                    [x * (gain_v[t, l, rows, j] * inc_v[t, l, rows, j]) for j, x in zip(runs, am)])

    def area(put, runs):
        for r in range(0, ROWS, 8):
            put(AREA, r, [ar_v[pl.ds(r, 8), j] for j in runs])

    def all_levels(what, put, runs):
        def two(i, _):
            what(put, runs, 2 * i)
            what(put, runs, 2 * i + 1)
            return 0

        lax.fori_loop(0, LEV // 2, two, 0)

    ends = [runs[0], runs[-1]]
    for c in loads[:4]:
        c.wait()
    area(edges, ends)
    all_levels(faces, edges, ends)
    near_top = la >= n_lat - 3

    @pl.when(near_top)
    def _():
        area(place, runs)
        all_levels(faces, place, runs)

    for c in loads[4:]:
        c.wait()
    all_levels(cells, edges, ends)

    lane8 = lanes_of((8, 128))

    def pack(i, _):
        rows = pl.ds(pl.multiple_of(i * 8, 8), 8)
        for p in range(PACKS):
            to_e = to_w = None
            for f in range(12 * p, min(12 * p + 12, FIELDS)):
                at = slot(f)[1]
                last = pltpu.roll(EDGE[f, 1, rows, :], (W + at) % 128, 1)
                first = EDGE[f, 0, rows, :]
                if at:
                    first = pltpu.roll(first, at, 1)
                to_e = last if to_e is None else jnp.where(lane8 >= at, last, to_e)
                to_w = first if to_w is None else jnp.where(lane8 >= at, first, to_w)
            P_[0, p, rows, :] = to_e
            P_[1, p, rows, :] = to_w
        return 0


    def remote(src, dst, ss, rs, dev):
        return pltpu.make_async_remote_copy(
            src_ref=src, dst_ref=dst, send_sem=ss, recv_sem=rs, device_id=dev, device_id_type=MESH
        )

    own_q = Q.at[0, :, pl.ds(M0, ROWS), :], Q.at[1, :, pl.ds(M0, ROWS), :]
    lon = [
        remote(P_.at[0], own_q[0], lon_s.at[0], lon_r.at[0], e_dev),
        remote(P_.at[1], own_q[1], lon_s.at[1], lon_r.at[1], w_dev),
    ]
    main = pl.ds(0, NT)
    low, high = pl.ds(M0, W), pl.ds(M1 - W, W)
    below, above = pl.ds(M0 - W, W), pl.ds(M1, W)
    parts = (pl.ds(KX, FIELDS - KX), pl.ds(0, KX))
    north = [remote(D.at[p, main, high, :], D.at[p, main, below, :], lat_s.at[0, i], lat_r.at[0, i], n_dev)
             for i, p in enumerate(parts)]
    south = [remote(D.at[p, main, low, :], D.at[p, main, above, :], lat_s.at[1, i], lat_r.at[1, i], s_dev)
             for i, p in enumerate(parts)]
    cor_n = remote(Q.at[:, :, high, :], Q.at[:, :, below, :], cor_s.at[0], cor_r.at[0], n_dev)
    cor_s_ = remote(Q.at[:, :, low, :], Q.at[:, :, above, :], cor_s.at[1], cor_r.at[1], s_dev)

    def share1(f, d):
        peer = mirror_dev(d)
        field = AREA if f == SHARE else n_lon * f + peer
        return remote(D.at[pl.ds(field, 1), main, high, :], F1.at[lo, pl.ds(f, 1), :, pl.ds(0, W), :],
                      f1_s.at[f, d], f1_r.at[f, d], (la, peer))

    def share2(f, d):
        peer = mirror_dev(d)
        return remote(F2.at[peer, pl.ds(f, 1), :, pl.ds(0, W), :], D.at[pl.ds(n_lon * f + lo, 1), :, above, :],
                      f2_s.at[f, d], f2_r.at[f, d], (la, peer))

    lax.fori_loop(0, ROWS // 8, pack, 0)

    pl.semaphore_wait(bar, jnp.where(is_top, n_lon, jnp.where(is_bottom, 3, 4)))

    for c in lon:
        c.start()

    @pl.when(~near_top)
    def _():
        area(place, runs)
        all_levels(faces, place, runs)

    @pl.when(is_top)
    def _():
        for d in range(1, n_lon):
            share1(2, d).start()

    all_levels(cells, place, runs)

    @pl.when(is_top)
    def _():
        for f in (1, 0, SHARE):
            for d in range(1, n_lon):
                share1(f, d).start()

    late_n = la == n_lat - 5

    @pl.when(not_top & ~late_n)
    def _():
        north[0].start()

    @pl.when(not_bottom)
    def _():
        south[0].start()

    @pl.when(is_top)
    def _():
        keep = [
            pltpu.make_async_copy(D.at[pl.ds(AREA if f == SHARE else n_lon * f + lo, 1), main, high, :],
                                  F1.at[lo, pl.ds(f, 1), :, pl.ds(0, W), :], f1_s.at[f, 0])
            for f in range(SHARE + 1)
        ]
        for c in keep:
            c.start()
        for c in keep:
            c.wait()

    @pl.when(is_bottom)
    def _():
        def clear(f, _):
            for ct in range(RING):
                for r in (M0 - W, M0 - 8):
                    D[f, ct, pl.ds(r, 8), :] = jnp.zeros((8, 128), F32)
            return 0

        lax.fori_loop(0, FIELDS, clear, 0)

    for c in range(NT):
        for r in range(M0, M1, 8):
            RA[c, pl.ds(r, 8), :] = 1.0 / D[AREA, c, pl.ds(r, 8), :]

    def unpack(r):
        for p in range(PACKS):
            w_side, e_side = Q[0, p, pl.ds(r, 8), :], Q[1, p, pl.ds(r, 8), :]
            for f in range(12 * p, min(12 * p + 12, FIELDS)):
                at = slot(f)[1]
                wv = pltpu.roll(w_side, (128 - W - at) % 128, 1)
                ev = pltpu.roll(e_side, (128 - at) % 128, 1) if at else e_side
                D[f, NT, pl.ds(r, 8), :] = jnp.where(lane8 < 64, ev, wv)

    def weights(chunks, fold):
        def levels(i, _):
            for l, r in itertools.product([LEVELS_AT_ONCE * i + q for q in range(LEVELS_AT_ONCE)], chunks):
                rows, up, down = pl.ds(r, 8), pl.ds(r + 1, 8), pl.ds(r - 1, 8)
                row = r + lax.broadcasted_iota(jnp.int32, (8, 128), 0)
                kx = [D[KX + l, ct, rows, :] for ct in range(RING)]
                m = [wet(x) for x in kx]
                ex = [k * n for k, n in zip(kx, east(m))]
                if fold:
                    ex = [jnp.where(row >= M1, k * n, x) for k, n, x in zip(east(kx), m, ex)]
                for ct, ew in enumerate(west(ex)):
                    ky, ky_s = D[KY + l, ct, rows, :], D[KY + l, ct, down, :]
                    m_n = wet(D[KX + l, ct, up, :])
                    yn, ys = ky * m_n, ky_s * m[ct]
                    if fold:
                        ky_n, m_s = D[KY + l, ct, up, :], wet(D[KX + l, ct, down, :])
                        yn_f, ys_f = ky_n * m[ct], ky * m_s
                        yn = jnp.where(row >= M1, yn_f, jnp.where(row == M1 - 1, 0.5 * (yn + yn_f), yn))
                        ys = jnp.where(row > M1, ys_f, jnp.where(row == M1, 0.5 * (ys + ys_f), ys))
                    a = D[AREA, ct, rows, :]
                    ce, cw, cn, cs = a * ex[ct], a * ew, a * yn, a * ys
                    CE[l, ct, rows, :], CW[l, ct, rows, :] = ce, cw
                    CN[l, ct, rows, :], CS[l, ct, rows, :] = cn, cs
                    C0[l, ct, rows, :] = 1.0 - ((ce + cw) + (cn + cs))
            return 0

        lax.fori_loop(0, LEV // LEVELS_AT_ONCE, levels, 0)

    H = (D, H1, H2, H3, H4, H5, H6, H7, H8, H9)

    def advance(k, chunks):
        src = H[k - 1]

        def levels(i, _):
            for q in range(LEVELS_AT_ONCE):
                l = LEVELS_AT_ONCE * i + q
                for r in chunks:
                    rows, up, down = pl.ds(r, 8), pl.ds(r + 1, 8), pl.ds(r - 1, 8)
                    cs = [[C[l, ct, rows, :] for C in (C0, CE, CW, CN, CS)] for ct in range(RING)]
                    for t in range(2):
                        f = t * LEV + l
                        h = [src[f, ct, rows, :] for ct in range(RING)]
                        he, hw = east(h), west(h)
                        new = []
                        for ct in range(RING if k < ITERS else NT):
                            c0, ce, cw, cn, c_s = cs[ct]
                            new.append((c0 * h[ct] + ce * he[ct]) + (
                                cw * hw[ct] + (cn * src[f, ct, up, :] + c_s * src[f, ct, down, :])))
                        if k < ITERS:
                            for ct in range(RING):
                                H[k][f, ct, rows, :] = new[ct]
                        else:
                            g = in_order([x * RA[ct, rows, :] for ct, x in enumerate(new)])
                            for j in range(NT):
                                O[t, l, j, pl.ds(r - M0, 8), :] = g[j]
            return 0

        lax.fori_loop(0, LEV // LEVELS_AT_ONCE, levels, 0)

    for c in lon:
        c.wait_recv()

    @pl.when(not_top)
    def _():
        cor_n.start()

    @pl.when(not_bottom)
    def _():
        cor_s_.start()
        south[1].start()

    @pl.when(not_top & ~late_n)
    def _():
        north[1].start()

    def unpack_own(i, _):
        unpack(M0 + pl.multiple_of(i * 8, 8))
        return 0

    lax.fori_loop(0, ROWS // 8, unpack_own, 0)
    weights(inner_rows(1), False)

    @pl.when(is_top)
    def _():
        pivot = part_s[0] + n_lon * COLS
        row_from = 7 - lax.broadcasted_iota(jnp.int32, (8, 128), 0)
        lane16 = lanes_of((16, 128))

        def counterpart(c):
            other = lax.rem(pivot - c, NT)
            at = (pivot - c - other) // NT
            return other, at // 128, lax.rem(at, 128)

        def turn(f):
            for s, c in itertools.product(range(n_lon), range(NT)):
                lanes = (counterpart(c)[2] - lane8) & 127
                for to, start in ((0, 2), (2, 0)):
                    x = jnp.take_along_axis(F1[s, f, c, pl.ds(start, 8), :], row_from, axis=0)
                    GG[f, s, c, pl.ds(to, 8), :] = take(x, lanes)

        def image(m, c, f):
            other, at, lane = counterpart(c)
            block = lax.rem(at - m + 2 * n_lon, n_lon)
            return jnp.where(lane16 <= lane, GG[f, block, other],
                             GG[f, lax.rem(block + n_lon - 1, n_lon), other])

        def halo(eastern, western):
            both = [jnp.where(lane16 < 64, e, w) for e, w in zip(eastern, western)]
            lanes = lane16 // NT + jnp.where(lane16 < 64, 0, 128 - GROUP)
            return pick([take(x, lanes) for x in both], lane16 % NT)

        for f in (2, 1, 0, SHARE):
            for d in range(1, n_lon):
                share1(f, d).wait_recv()
            turn(f)
            if f == SHARE:
                for c in range(NT):
                    D[AREA, c, above, :] = image(lo, c, SHARE)[:W]
                e, w = lax.rem(lo + 1, n_lon), lax.rem(lo + n_lon - 1, n_lon)
                D[AREA, NT, above, :] = halo([image(e, c, SHARE) for c in range(NT)],
                                             [image(w, c, SHARE) for c in range(NT)])[:W]
                continue
            for m, c in itertools.product(range(n_lon), range(NT)):
                F2[m, f, c] = image(m, c, f)
            for m in range(n_lon):
                e, w = (m + 1) % n_lon, (m - 1) % n_lon
                F2[m, f, NT] = halo([F2[e, f, c] for c in range(NT)], [F2[w, f, c] for c in range(NT)])
            for d in range(1, n_lon):
                share2(f, d).start()
        keep = [
            pltpu.make_async_copy(F2.at[lo, pl.ds(f, 1), :, pl.ds(0, W), :],
                                  D.at[pl.ds(n_lon * f + lo, 1), :, above, :], f2_s.at[f, 0])
            for f in range(SHARE)
        ]
        for c in keep:
            c.start()
        for c in keep:
            c.wait()

    for k in range(1, ITERS + 1):
        advance(k, inner_rows(k))

    @pl.when(late_n)
    def _():
        north[0].start()

    def side(i, _):
        northern = i == lax.rem(la, 2)
        southern = i != lax.rem(la, 2)

        @pl.when(late_n & (i == 1))
        def _():
            north[1].start()

        @pl.when(southern & not_bottom)
        def _():
            cor_n.wait_recv()
            for r in (M0 - W, M0 - 8):
                unpack(r)
            north[0].wait_recv()

        @pl.when(southern)
        def _():
            weights((M0 - W + 1, M0 - 7), False)

        @pl.when(southern & not_bottom)
        def _():
            north[1].wait_recv()

        @pl.when(southern)
        def _():
            for k in range(1, ITERS + 1):
                advance(k, (M0 - W + k, M0 - 8 + k))

        @pl.when(northern & not_top)
        def _():
            cor_s_.wait_recv()
            for r in (M1, M1 + W - 8):
                unpack(r)
            south[0].wait_recv()
            weights((M1 - 1, M1 + W - 9), False)
            south[1].wait_recv()

        @pl.when(northern & is_top)
        def _():
            for f in range(SHARE - 1, 0, -1):
                for d in range(1, n_lon):
                    share2(f, d).wait_recv()
            weights((M1 - 1, M1 + W - 9), True)
            for d in range(1, n_lon):
                share2(0, d).wait_recv()

        @pl.when(northern)
        def _():
            for k in range(1, ITERS + 1):
                advance(k, (M1 - k, M1 + W - 8 - k))

        return 0

    lax.fori_loop(0, 2, side, 0)
    results = [
        pltpu.make_async_copy(O.at[:, :, j], out.at[:, :, :, pl.ds(128 * j, 128)], out_sem.at[j])
        for j in range(NT)
    ]
    for c in results:
        c.start()

    for c in lon:
        c.wait_send()

    @pl.when(not_top)
    def _():
        for c in north:
            c.wait_send()
        cor_n.wait_send()

    @pl.when(not_bottom)
    def _():
        for c in south:
            c.wait_send()
        cor_s_.wait_send()

    @pl.when(is_top)
    def _():
        for d in range(1, n_lon):
            for f in range(SHARE + 1):
                share1(f, d).wait_send()
            for f in range(SHARE):
                share2(f, d).wait_send()

    for c in results:
        c.wait()


def on_device(n_lat, n_lon, *args):
    vmem = lambda *shape: pltpu.VMEM(shape, F32)
    dma = lambda *shape: pltpu.SemaphoreType.DMA(shape)
    scratch = [
        vmem(2, LEV, ROWS, COLS), vmem(2, LEV, ROWS, COLS), vmem(LEV, ROWS, COLS), vmem(LEV, ROWS, COLS),
        pltpu.VMEM((LEV, ROWS, COLS), jnp.int32), vmem(ROWS, COLS), pltpu.SMEM((1024,), jnp.int32),
        vmem(FIELDS, RING, HEIGHT, 128), *[vmem(2 * LEV, RING, HEIGHT, 128)] * (ITERS - 1),
        *[vmem(LEV, RING, HEIGHT, 128)] * 5, vmem(NT, HEIGHT, 128), vmem(2, LEV, NT, ROWS, 128),
        vmem(FIELDS, 2, ROWS, 128), vmem(2, PACKS, ROWS, 128), vmem(2, PACKS, HEIGHT, 128),
        vmem(n_lon, SHARE + 1, NT, 16, 128), vmem(SHARE + 1, n_lon, NT, 16, 128),
        vmem(n_lon, SHARE, RING, 16, 128),
        dma(7), dma(NT), dma(2, 2), dma(2, 2), dma(2), dma(2), dma(2), dma(2),
        dma(SHARE + 1, n_lon), dma(SHARE + 1, n_lon), dma(SHARE, n_lon), dma(SHARE, n_lon),
    ]
    return pl.pallas_call(
        functools.partial(kernel, n_lat, n_lon),
        out_shape=jax.ShapeDtypeStruct((2, LEV, ROWS, COLS), F32),
        in_specs=[pl.BlockSpec(memory_space=pl.ANY)] * 7,
        out_specs=pl.BlockSpec(memory_space=pl.ANY),
        scratch_shapes=scratch,
        compiler_params=pltpu.CompilerParams(
            collective_id=0, has_side_effects=True, vmem_limit_bytes=60 * 2**20
        ),
    )(*args)


def solution(mesh):
    in_specs = (
        P(None, None, "lat", "lon"),
        P(None, None, "lat", "lon"),
        P(None, "lat", "lon"),
        P(None, "lat", "lon"),
        P(None, "lat", "lon"),
        P("lat", "lon"),
        P(),
    )
    out_specs = P(None, None, "lat", "lon")
    return jax.shard_map(
        functools.partial(on_device, mesh.shape["lat"], mesh.shape["lon"]),
        mesh=mesh, in_specs=in_specs, out_specs=out_specs, check_vma=False,
    )
```
